32 devices in a mesh: rep: 2 (over y), gx: 4 (over z), yz: 4 (over x, core).
Axes of the slice: x: 2, y: 2, z: 4, core: 2. Of those that a mesh axis runs over, the one named last changes fastest.
Arguments:
- inputs: bfloat16 [1024, 8192], P('rep', ('gx', 'yz')), parts along dimension 0, may hold values from -6 to 6
- gate_weight: bfloat16 [8192, 26624], P('gx', 'yz'), may hold values from -0.09375 to 0.09375
- up_weight: bfloat16 [8192, 26624], P('gx', 'yz'), may hold values from -0.0625 to 0.0625
- down_weight: bfloat16 [26624, 8192], P('yz', 'gx'), may hold values from -0.0546875 to 0.0546875
Outputs:
- mixed: bfloat16 [1024, 8192], P('rep', ('gx', 'yz')), parts along dimension 0
The draws below stay inside these ranges and needn't reach their ends.
There are 2 independent parts, one for each index of `rep`. The reference program is written for one: setup_inputs(seed, part) draws one part's arguments, and reference() takes and returns one part's arrays. A program takes and returns all parts, laid end to end along the dimension named above; an argument that names none is the same for every part. Nothing has to cross between parts.
All inputs are finite; a program needn't handle non-finite values.
Results may differ from the reference program's by a relative error of at most 0.019.
Values may be sent and summed in bfloat16 or wider, within the bound.
No kernel may reach another device: no remote copies, remote signals or barrier semaphores. Data moves between devices by JAX's collectives and lax.ppermute only.
A program may use at most 256 MiB of HBM per device.

```python
import jax
import jax.numpy as jnp
from jax import lax

D = 8192
FF = 26624
ROWS = 512
N_GX = 4


def with_spikes(array, own_key, source, target, parts, factor):
    owner, partner = [(jnp.arange(array.shape[position]) // (array.shape[position] // parts)).reshape([-1 if axis == position else 1 for axis in range(array.ndim)]) for position in (source, target)]
    chosen = jax.random.permutation(own_key, parts)[partner]
    strong = (owner == chosen) | (owner == (partner + parts // 2) % parts)
    return jnp.where(strong, factor * array, array)


def shard_levels(own_key, shape, cuts, low, top_value):
    level, own = 1.0, jax.random.fold_in(own_key, 6)
    for position, parts in cuts:
        steps = jnp.exp(jax.random.uniform(jax.random.fold_in(own, position), (parts,), jnp.float32, low / len(cuts), top_value / len(cuts)))
        level = level * jnp.repeat(steps, shape[position] // parts).reshape([-1 if axis == position else 1 for axis in range(len(shape))])
    return level


def gaussian(own_key, shape, scale, limit, split=(), held_as=jnp.bfloat16):
    array = jax.random.normal(own_key, shape, jnp.float32) * scale
    if len(split) > 0:
        array = shard_levels(own_key, shape, split, -0.22, 0.18) * array
    return jnp.clip(array, min=-limit, max=limit).astype(held_as)


def bell_draw_with(rng, shape, scale, reach, shards, heavy, held_as=jnp.bfloat16):
    array = scale * jax.random.normal(rng, shape, jnp.float32)
    if shards:
        array = array * shard_levels(rng, shape, shards, -0.22, 0.18)
    return jnp.clip(with_spikes(array, jax.random.fold_in(rng, 3), *heavy), -reach, reach).astype(held_as)


def setup_inputs(seed: int = 0, part: int = 0) -> dict:
    seeds = jax.random.split(jax.random.key(seed), 5)
    part_splits = jax.random.split(jax.random.fold_in(seeds[4], part), 5)
    inputs = gaussian(part_splits[0], (ROWS, D), 1.0, 6.0, ((1, 16),))
    gate_weight = bell_draw_with(seeds[1], (D, FF), D ** -0.5, 0.09375, ((0, 4), (1, 4)), (0, 1, 4, 2.0))
    up_weight = gaussian(seeds[2], (D, FF), D ** -0.5, 0.0625, ((0, 4), (1, 4)))
    down_weight = bell_draw_with(seeds[3], (FF, D), FF ** -0.5, 0.0546875, ((0, 4), (1, 4)), (0, 1, 4, 2.0))
    return dict(inputs=inputs, gate_weight=gate_weight, up_weight=up_weight, down_weight=down_weight)


def reference(inputs, gate_weight, up_weight, down_weight):
    width = D // N_GX
    blocks = inputs.reshape(ROWS, N_GX, width).transpose(1, 0, 2)
    gate_blocks = gate_weight.reshape(N_GX, width, FF)
    up_blocks = up_weight.reshape(N_GX, width, FF)

    def accumulate(carry, item):
        piece, gate_rows, up_rows = item
        gate_term = jnp.dot(piece, gate_rows, preferred_element_type=jnp.float32).astype(jnp.bfloat16)
        up_term = jnp.dot(piece, up_rows, preferred_element_type=jnp.float32).astype(jnp.bfloat16)
        gate_term, up_term = lax.optimization_barrier((gate_term, up_term))
        return (carry[0] + gate_term.astype(jnp.float32), carry[1] + up_term.astype(jnp.float32)), None

    start = (jnp.zeros((ROWS, FF), jnp.float32), jnp.zeros((ROWS, FF), jnp.float32))
    (gate, up), unused = lax.scan(accumulate, start, (blocks, gate_blocks, up_blocks))
    hidden = (jax.nn.silu(gate) * up).astype(jnp.bfloat16)
    return jnp.dot(hidden, down_weight, preferred_element_type=jnp.float32).astype(jnp.bfloat16)
```

```python
import functools

import jax
import jax.numpy as jnp
from jax import lax
from jax.sharding import PartitionSpec as P

WIDTH = 384


def choose(index, cases):
    if all(case is cases[0] for case in cases):
        return cases[0]
    return lax.select_n(index, *cases)


def gather_features(own, index, count):
    pair = [(i, i ^ 1) for i in range(count)]
    chips = count // 2
    core, chip = index % 2, index // 2
    far = [own]
    for _ in range(chips - 1):
        far.append(lax.ppermute(far[-1], "yz", [(i, (i + 2) % count) for i in range(count)]))
    near = [lax.ppermute(block, "yz", pair) for block in far]
    blocks = []
    for j in range(chips):
        mine = choose(chip, [far[(v - j) % chips] for v in range(chips)])
        other = choose(chip, [near[(v - j) % chips] for v in range(chips)])
        blocks += [choose(core, [mine, other]), choose(core, [other, mine])]
    return lax.concatenate(blocks, 1)


def scatter_sum(partial, index, count):
    rows, total = partial.shape
    share = total // count
    chips = count // 2
    core, chip = index % 2, index // 2
    blocks = partial.reshape(rows, chips, 2, share)
    blocks = [[blocks[:, j, c] for c in range(2)] for j in range(chips)]
    keep = [choose(core, [b[0], b[1]]) for b in blocks]
    give = lax.concatenate([choose(core, [b[1], b[0]]) for b in blocks], 1)
    got = lax.ppermute(give, "yz", [(i, i ^ 1) for i in range(count)])
    sums = [
        (k.astype(jnp.float32) + got[:, j * share : (j + 1) * share].astype(jnp.float32)).astype(jnp.bfloat16)
        for j, k in enumerate(keep)
    ]
    result = choose(chip, sums).astype(jnp.float32)
    for k in range(1, chips):
        send = choose(chip, [sums[(v + k) % chips] for v in range(chips)])
        moved = lax.ppermute(send, "yz", [(i, (i + 2 * k) % count) for i in range(count)])
        result = result + moved.astype(jnp.float32)
    return result.astype(jnp.bfloat16)


def shards(inputs, gate_weight, up_weight, down_weight, *, n, count):
    z = lax.axis_index("gx")
    index = lax.axis_index("yz")
    back = n - 1 - z
    rows = inputs.shape[0]
    half = gate_weight.shape[1] // 2
    w = WIDTH
    chunks = -(-half // w)
    starts = [min(c * w, half - w) for c in range(chunks)]
    sends = -(-chunks // 2)
    first = max([chunks] + [min(2 * k + 1, chunks - 1) + n - 1 - k for k in range(sends)])
    slots = first + sends + n - 2
    up_pairs = [(i, i + 1) for i in range(n - 1)]
    down_pairs = [(i + 1, i) for i in range(n - 1)]
    zeros = jnp.zeros((rows, 2 * w), jnp.bfloat16)

    whole = gather_features(inputs, index, count)

    def part(start):
        return lax.concatenate(
            [
                jnp.dot(
                    whole, weight[:, start : start + w], preferred_element_type=jnp.float32
                ).astype(jnp.bfloat16)
                for weight in (gate_weight, up_weight)
            ],
            1,
        )

    low = [part(start) for start in starts]
    high = [part(half + start) for start in starts]

    from_below, from_above, hidden, packed = {}, {}, {}, {}
    total = None

    def make_hidden(c):
        got = choose((z > 0).astype(jnp.int32), [from_above[c + n - 2], from_below[c + n - 2]])
        own = choose((z > 0).astype(jnp.int32), [low[c], high[c]])
        both = got.astype(jnp.float32) + own.astype(jnp.float32)
        return (jax.nn.silu(both[:, :w]) * both[:, w:]).astype(jnp.bfloat16)

    def addend(slot, place, parts):
        c = slot - place
        if c < chunks:
            return parts[max(c, 0)]
        k = c - first
        if place == 0 and 0 <= k < sends:
            return packed[k]
        return zeros

    for slot in range(slots):
        up = choose(z, [addend(slot, min(v, n - 2), high) for v in range(n)])
        down = choose(back, [addend(slot, min(v, n - 2), low) for v in range(n)])
        if slot > 0:
            up = up + from_below[slot - 1]
            down = down + from_above[slot - 1]
        up, down = lax.optimization_barrier((up, down))
        from_below[slot] = lax.ppermute(up, "gx", up_pairs)
        from_above[slot] = lax.ppermute(down, "gx", down_pairs)

        c = slot - (n - 2)
        if 0 <= c < chunks:
            hidden[c] = make_hidden(c)
            if c % 2 == 1 or c == chunks - 1:
                k = c // 2
                new = half - c * w
                last = hidden[c] if new >= w else hidden[c][:, w - new :]
                pieces = [hidden[c - 1], last] if c % 2 == 1 else [last]
                width = sum(p.shape[1] for p in pieces)
                if width < 2 * w:
                    pieces.append(zeros[:, : 2 * w - width])
                packed[k] = lax.concatenate(pieces, 1)

        k = slot - (first + n - 2)
        if 0 <= k < sends:
            width = min(2 * w, half - 2 * k * w)
            lower = choose(z, [packed[k]] + [from_below[first + k + v] for v in range(n - 1)])
            upper = choose(back, [packed[k]] + [from_above[first + k + v] for v in range(n - 1)])
            at = 2 * k * w
            for rows_of, offset in ((lower, at), (upper, half + at)):
                term = jnp.dot(
                    rows_of[:, :width],
                    down_weight[offset : offset + width],
                    preferred_element_type=jnp.float32,
                )
                total = term if total is None else total + term

    return scatter_sum(total.astype(jnp.bfloat16), index, count)


def solution(mesh):
    return jax.shard_map(
        functools.partial(shards, n=mesh.shape["gx"], count=mesh.shape["yz"]),
        mesh=mesh,
        in_specs=(P("rep", ("gx", "yz")), P("gx", "yz"), P("gx", "yz"), P("yz", "gx")),
        out_specs=P("rep", ("gx", "yz")),
        check_vma=False,
    )
```

```python
import functools

import jax
import jax.numpy as jnp
from jax import lax
from jax.experimental import pallas as pl
from jax.experimental.pallas import tpu as pltpu
from jax.sharding import PartitionSpec as P

LANES = 128
UNITS = 3


def choose(index, cases):
    if all(case is cases[0] for case in cases):
        return cases[0]
    return lax.select_n(index, *cases)


def gather_features(own, index, count):
    pair = [(i, i ^ 1) for i in range(count)]
    chips = count // 2
    core, chip = index % 2, index // 2
    far = [own]
    for _ in range(chips - 1):
        far.append(lax.ppermute(far[-1], "yz", [(i, (i + 2) % count) for i in range(count)]))
    near = [lax.ppermute(block, "yz", pair) for block in far]
    blocks = []
    for j in range(chips):
        mine = choose(chip, [far[(v - j) % chips] for v in range(chips)])
        other = choose(chip, [near[(v - j) % chips] for v in range(chips)])
        blocks += [choose(core, [mine, other]), choose(core, [other, mine])]
    return lax.concatenate(blocks, 1)


def scatter_sum(partial, index, count):
    rows, total = partial.shape
    share = total // count
    chips = count // 2
    core, chip = index % 2, index // 2
    blocks = partial.reshape(rows, chips, 2, share)
    blocks = [[blocks[:, j, c] for c in range(2)] for j in range(chips)]
    keep = [choose(core, [b[0], b[1]]) for b in blocks]
    give = lax.concatenate([choose(core, [b[1], b[0]]) for b in blocks], 1)
    got = lax.ppermute(give, "yz", [(i, i ^ 1) for i in range(count)])
    sums = [
        (k.astype(jnp.float32) + got[:, j * share : (j + 1) * share].astype(jnp.float32)).astype(jnp.bfloat16)
        for j, k in enumerate(keep)
    ]
    result = choose(chip, sums).astype(jnp.float32)
    for k in range(1, chips):
        send = choose(chip, [sums[(v + k) % chips] for v in range(chips)])
        moved = lax.ppermute(send, "yz", [(i, (i + 2 * k) % count) for i in range(count)])
        result = result + moved.astype(jnp.float32)
    return result.astype(jnp.bfloat16)


def first_dots(features, gate_weight, up_weight, start, units):
    rows, depth = features.shape

    def kernel(x_ref, gate_ref, up_ref, low_ref, high_ref):
        gate = jnp.dot(x_ref[...], gate_ref[...], preferred_element_type=jnp.float32).astype(jnp.bfloat16)
        low_ref[:, :LANES] = gate[:, :LANES]
        high_ref[:, :LANES] = gate[:, LANES:]
        up = jnp.dot(x_ref[...], up_ref[...], preferred_element_type=jnp.float32).astype(jnp.bfloat16)
        low_ref[:, LANES:] = up[:, :LANES]
        high_ref[:, LANES:] = up[:, LANES:]

    weight = pl.BlockSpec((depth, 2 * LANES), lambda j: (0, start + j))
    out = pl.BlockSpec((rows, 2 * LANES), lambda j: (0, j))
    wide = 2 * LANES * units
    return pl.pallas_call(
        kernel,
        grid=(units,),
        in_specs=[pl.BlockSpec((rows, depth), lambda j: (0, 0)), weight, weight],
        out_specs=[out, out],
        out_shape=[jax.ShapeDtypeStruct((rows, wide), jnp.bfloat16)] * 2,
        compiler_params=pltpu.CompilerParams(vmem_limit_bytes=32 * 1024 * 1024),
        cost_estimate=pl.CostEstimate(
            flops=4 * rows * depth * wide,
            bytes_accessed=2 * (rows * depth + 2 * depth * wide + 2 * rows * wide),
            transcendentals=0,
        ),
    )(features, gate_weight, up_weight)


def shards(inputs, gate_weight, up_weight, down_weight, *, n, count):
    z = lax.axis_index("gx")
    index = lax.axis_index("yz")
    core = index % 2
    back = n - 1 - z
    inner = (z > 0).astype(jnp.int32)
    rows = inputs.shape[0]
    units = gate_weight.shape[1] // (2 * LANES)
    runs = ([units % UNITS] if units % UNITS else []) + [UNITS] * (units // UNITS)
    chunks = len(runs)
    starts = [sum(runs[:c]) for c in range(chunks)]

    late = max(chunks - 3, 0) // 2 * 2
    pieces = [([c, c + 1], 0, rows) for c in range(0, late, 2)]
    tail = list(range(late, chunks))
    pieces += [(tail, 0, rows // 2), (tail, rows // 2, rows)]
    sends = len(pieces)
    first = max([chunks] + [piece[0][-1] + n - 1 - k for k, piece in enumerate(pieces)])
    slots = first + sends + n - 2
    up_pairs = [(i, i + 1) for i in range(n - 1)]
    down_pairs = [(i + 1, i) for i in range(n - 1)]

    def size(members):
        return LANES * sum(runs[m] for m in members)

    def shape_of(slot):
        active = [slot - v for v in range(n - 1)]
        wide = [2 * size([c]) for c in active if 0 <= c < chunks]
        wide += [size(pieces[c - first][0]) for c in active if 0 <= c - first < sends - 2]
        if wide:
            last = sum(0 <= c - first - sends + 2 < 2 for c in active)
            return (rows, max(wide + ([-(-size(tail) // 2)] if last else [])))
        return (rows // 2, size(tail))

    def fit(array, shape):
        if array.shape[0] == shape[0]:
            extra = shape[1] - array.shape[1]
            if extra > 0:
                return jnp.pad(array, ((0, 0), (0, extra)))
            return array[:, : shape[1]] if extra < 0 else array
        top = rows // 2
        if array.shape[0] < shape[0]:
            rest = array[:, shape[1] :]
            rest = jnp.pad(rest, ((0, 0), (0, shape[1] - rest.shape[1])))
            return lax.concatenate([array[:, : shape[1]], rest], 0)
        return lax.concatenate([array[:top], array[top:, : shape[1] - array.shape[1]]], 1)

    low, high = {}, {}
    from_below, from_above, hidden, packed, terms = {}, {}, {}, {}, {}
    total, results = None, []

    def make_hidden(c):
        got = choose(inner, [from_above[c + n - 2], from_below[c + n - 2]])
        own = choose(inner, [low[c], high[c]])
        sums = got[:, : 2 * size([c])].astype(jnp.float32) + own.astype(jnp.float32)
        columns = [sums[:, LANES * i : LANES * (i + 1)] for i in range(2 * runs[c])]
        gate = lax.concatenate(columns[::2], 1)
        up = lax.concatenate(columns[1::2], 1)
        return (jax.nn.silu(gate) * up).astype(jnp.bfloat16)

    def addend(slot, place, parts, shape):
        c = slot - place
        if c < chunks:
            return fit(parts[max(c, 0)], shape)
        k = c - first
        if place == 0 and 0 <= k < sends:
            return fit(packed[k], shape)
        return jnp.zeros(shape, jnp.bfloat16)

    whole = gather_features(inputs, index, count)

    def dots(whole, c):
        return tuple(first_dots(whole, gate_weight, up_weight, starts[c], runs[c]))

    low[0], high[0] = dots(whole, 0)
    early = lax.cond(
        core == 0,
        lambda w: dots(w, 1),
        lambda w: (jnp.zeros((rows, 2 * size([1])), jnp.bfloat16),) * 2,
        whole,
    )
    whole, low[0], high[0], early = lax.optimization_barrier((whole, low[0], high[0], early))
    for slot in range(slots):
        shape = shape_of(slot)
        up = choose(z, [addend(slot, min(v, n - 2), high, shape) for v in range(n)])
        down = choose(back, [addend(slot, min(v, n - 2), low, shape) for v in range(n)])
        if slot > 0:
            up = up + fit(from_below[slot - 1], shape)
            down = down + fit(from_above[slot - 1], shape)
        tied = terms.pop(slot - 2, None)
        whole, up, down, tied = lax.optimization_barrier((whole, up, down, tied))
        if tied is not None:
            total = tied if total is None else total + tied
        from_below[slot] = lax.ppermute(up, "gx", up_pairs)
        from_above[slot] = lax.ppermute(down, "gx", down_pairs)
        if slot == 0:
            low[1], high[1] = lax.cond(core == 0, lambda w, e: e, lambda w, e: dots(w, 1), whole, early)
        elif slot + 1 < chunks:
            low[slot + 1], high[slot + 1] = dots(whole, slot + 1)

        c = slot - (n - 2)
        if 0 <= c < chunks:
            hidden[c] = make_hidden(c)
            for k, (members, top, bottom) in enumerate(pieces):
                if members[-1] == c:
                    packed[k] = lax.concatenate([hidden[m][top:bottom] for m in members], 1)

        k = slot - (first + n - 2)
        if 0 <= k < sends:
            members, top, bottom = pieces[k]
            shape = packed[k].shape
            lower = choose(z, [packed[k]] + [fit(from_below[first + k + v], shape) for v in range(n - 1)])
            upper = choose(back, [packed[k]] + [fit(from_above[first + k + v], shape) for v in range(n - 1)])
            parts = []
            for i in range(shape[1] // LANES):
                parts += [block[:, LANES * i : LANES * (i + 1)] for block in (lower, upper)]
            at = 2 * LANES * starts[members[0]]
            term = jnp.dot(
                lax.concatenate(parts, 1),
                down_weight[at : at + 2 * shape[1]],
                preferred_element_type=jnp.float32,
            )
            if bottom - top == rows:
                terms[slot] = term
            else:
                for other in [*terms.values(), *([] if total is None else [total])]:
                    term = term + other[top:bottom]
                results.append(scatter_sum(term.astype(jnp.bfloat16), index, count))
    return lax.concatenate(results, 0)


def solution(mesh):
    return jax.shard_map(
        functools.partial(shards, n=mesh.shape["gx"], count=mesh.shape["yz"]),
        mesh=mesh,
        in_specs=(P("rep", ("gx", "yz")), P("gx", "yz"), P("gx", "yz"), P("yz", "gx")),
        out_specs=P("rep", ("gx", "yz")),
        check_vma=False,
    )
```

```python
import functools

import jax
import jax.numpy as jnp
from jax import lax
from jax.experimental import pallas as pl
from jax.experimental.pallas import tpu as pltpu
from jax.sharding import PartitionSpec as P

LANES = 128
UNITS = 3


def choose(index, cases):
    if all(case is cases[0] for case in cases):
        return cases[0]
    return lax.select_n(index, *cases)


def gather_features(own, index, count):
    pair = [(i, i ^ 1) for i in range(count)]
    chips = count // 2
    core, chip = index % 2, index // 2
    far = [own]
    for _ in range(chips - 1):
        far.append(lax.ppermute(far[-1], "yz", [(i, (i + 2) % count) for i in range(count)]))
    near = [lax.ppermute(block, "yz", pair) for block in far]
    blocks = []
    for j in range(chips):
        mine = choose(chip, [far[(v - j) % chips] for v in range(chips)])
        other = choose(chip, [near[(v - j) % chips] for v in range(chips)])
        blocks += [choose(core, [mine, other]), choose(core, [other, mine])]
    return lax.concatenate(blocks, 1)


def spread_units(lower_ref, upper_ref, held_ref):
    for i in range(lower_ref.shape[1] // LANES):
        held_ref[:, 2 * LANES * i : 2 * LANES * i + LANES] = lower_ref[:, LANES * i : LANES * (i + 1)]
        held_ref[:, 2 * LANES * i + LANES : 2 * LANES * (i + 1)] = upper_ref[:, LANES * i : LANES * (i + 1)]


def down_dots(lower, upper, down_weight, base, start):
    rows, size = lower.shape
    total = down_weight.shape[1]
    depth, wide = 2 * size, min(total, 4 * LANES)

    def kernel(lower_ref, upper_ref, weight_ref, *refs):
        out_ref, held_ref = refs[-2:]

        @pl.when(pl.program_id(0) == 0)
        def _():
            spread_units(lower_ref, upper_ref, held_ref)

        term = jnp.dot(held_ref[...], weight_ref[...], preferred_element_type=jnp.float32)
        out_ref[...] = term + refs[0][...] if len(refs) > 2 else term

    here = pl.BlockSpec((rows, size), lambda step: (0, 0))
    block = pl.BlockSpec((rows, wide), lambda step: (0, step))
    weight = pl.BlockSpec((pl.Element(depth), pl.Element(wide)), lambda step: (start, step * wide))
    given = [] if base is None else [base]
    return pl.pallas_call(
        kernel,
        grid=(total // wide,),
        in_specs=[here, here, weight] + [block] * len(given),
        out_specs=block,
        out_shape=jax.ShapeDtypeStruct((rows, total), jnp.float32),
        scratch_shapes=[pltpu.VMEM((rows, depth), jnp.bfloat16)],
        compiler_params=pltpu.CompilerParams(vmem_limit_bytes=40 * 1024 * 1024),
        cost_estimate=pl.CostEstimate(flops=0, bytes_accessed=0, transcendentals=0),
    )(lower, upper, down_weight, *given)


def last_dots(lower, upper, down_weight, base, place, start, block):
    rows, size = lower.shape
    total = down_weight.shape[1]
    depth, wide = 2 * size, total // place.shape[0]
    steps = place.shape[0]

    def kernel(place_ref, lower_ref, upper_ref, weight_ref, base_ref, give_ref, keep_ref, held_ref):
        spread_units(lower_ref, upper_ref, held_ref)
        for step in range(steps):
            columns = pl.ds(pl.multiple_of(place_ref[step] * wide, wide), wide)
            term = jnp.dot(held_ref[...], weight_ref[:, columns], preferred_element_type=jnp.float32)
            result = (term + base_ref[:, columns]).astype(jnp.bfloat16)
            out_ref, at = (give_ref, step) if step < steps // 2 else (keep_ref, step - steps // 2)
            out_ref[:, wide * at : wide * (at + 1)] = result

    here = pl.BlockSpec((rows, size), lambda i, place: (0, 0))
    out = pl.BlockSpec((rows, total // 2), lambda i, place: (0, 0))
    return pl.pallas_call(
        kernel,
        grid_spec=pltpu.PrefetchScalarGridSpec(
            num_scalar_prefetch=1,
            grid=(1,),
            in_specs=[
                here,
                here,
                pl.BlockSpec((pl.Element(depth), pl.Element(total)), lambda i, place: (start, 0)),
                pl.BlockSpec((rows, total), lambda i, place: (block, 0)),
            ],
            out_specs=[out, out],
            scratch_shapes=[pltpu.VMEM((rows, depth), jnp.bfloat16)],
        ),
        out_shape=[jax.ShapeDtypeStruct((rows, total // 2), jnp.bfloat16)] * 2,
        compiler_params=pltpu.CompilerParams(vmem_limit_bytes=40 * 1024 * 1024),
        cost_estimate=pl.CostEstimate(
            flops=2 * rows * depth * total, bytes_accessed=2 * depth * total + 6 * rows * total, transcendentals=0
        ),
    )(place, lower, upper, down_weight, base)


def split_columns(total, core, count):
    share = total.shape[1] // count
    blocks = [total[:, share * i : share * (i + 1)].astype(jnp.bfloat16) for i in range(count)]
    return [
        lax.concatenate([choose(c, [blocks[2 * j], blocks[2 * j + 1]]) for j in range(count // 2)], 1)
        for c in (1 - core, core)
    ]


def chip_sums(give, keep, count):
    got = lax.ppermute(give, "yz", [(i, i ^ 1) for i in range(count)])
    return (keep.astype(jnp.float32) + got.astype(jnp.float32)).astype(jnp.bfloat16)


def scatter_chips(sums, chip, count):
    chips = count // 2
    share = sums.shape[1] // chips
    blocks = [sums[:, share * j : share * (j + 1)] for j in range(chips)]
    return [choose(chip, [blocks[(v + k) % chips] for v in range(chips)]) for k in range(chips)]


def add_chips(sends, count):
    result = sends[0].astype(jnp.float32)
    for k, send in enumerate(sends[1:], 1):
        moved = lax.ppermute(send, "yz", [(i, (i + 2 * k) % count) for i in range(count)])
        result = result + moved.astype(jnp.float32)
    return result.astype(jnp.bfloat16)


def first_dots(features, gate_weight, up_weight, start, units):
    rows, depth = features.shape

    def kernel(x_ref, gate_ref, up_ref, low_ref, high_ref):
        gate = jnp.dot(x_ref[...], gate_ref[...], preferred_element_type=jnp.float32).astype(jnp.bfloat16)
        low_ref[:, :LANES] = gate[:, :LANES]
        high_ref[:, :LANES] = gate[:, LANES:]
        up = jnp.dot(x_ref[...], up_ref[...], preferred_element_type=jnp.float32).astype(jnp.bfloat16)
        low_ref[:, LANES:] = up[:, :LANES]
        high_ref[:, LANES:] = up[:, LANES:]

    weight = pl.BlockSpec((depth, 2 * LANES), lambda j: (0, start + j))
    out = pl.BlockSpec((rows, 2 * LANES), lambda j: (0, j))
    wide = 2 * LANES * units
    return pl.pallas_call(
        kernel,
        grid=(units,),
        in_specs=[pl.BlockSpec((rows, depth), lambda j: (0, 0)), weight, weight],
        out_specs=[out, out],
        out_shape=[jax.ShapeDtypeStruct((rows, wide), jnp.bfloat16)] * 2,
        compiler_params=pltpu.CompilerParams(vmem_limit_bytes=32 * 1024 * 1024),
        cost_estimate=pl.CostEstimate(
            flops=0,
            bytes_accessed=0,
            transcendentals=0,
        ),
    )(features, gate_weight, up_weight)


def shards(inputs, gate_weight, up_weight, down_weight, *, n, count):
    index = lax.axis_index("yz")
    core = index % 2
    z = lax.axis_index("gx")
    back = n - 1 - z
    inner = (z > 0).astype(jnp.int32)
    rows = inputs.shape[0]
    units = gate_weight.shape[1] // (2 * LANES)
    runs = ([units % UNITS] if units % UNITS else []) + [UNITS] * (units // UNITS)
    chunks = len(runs)
    starts = [sum(runs[:c]) for c in range(chunks)]
    pieces = [list(range(c, min(c + 2, chunks))) for c in range(0, chunks, 2)]
    sends = len(pieces)
    first = max([chunks] + [piece[-1] + n - 1 - k for k, piece in enumerate(pieces)])
    slots = first + sends + n - 2
    up_pairs = [(i, i + 1) for i in range(n - 1)]
    down_pairs = [(i + 1, i) for i in range(n - 1)]

    def size(members):
        return LANES * sum(runs[m] for m in members)

    def width(slot):
        active = [slot - v for v in range(n - 1)]
        wide = [2 * size([c]) for c in active if 0 <= c < chunks]
        wide += [size(pieces[c - first]) for c in active if 0 <= c - first < sends]
        return max(wide)

    def fit(array, wide):
        if array.shape[1] < wide:
            return jnp.pad(array, ((0, 0), (0, wide - array.shape[1])))
        return array[:, :wide]

    low, high = {}, {}
    from_below, from_above, packed, terms, hidden = {}, {}, {}, {}, {}
    results = []
    place = jnp.stack([2 * j + c for c in (1 - core, core) for j in range(count // 2)]).astype(jnp.int32)

    def make_hidden(c):
        got = choose(inner, [from_above[c + n - 2], from_below[c + n - 2]])
        own = choose(inner, [low[c], high[c]])
        sums = got[:, : 2 * size([c])].astype(jnp.float32) + own.astype(jnp.float32)
        columns = [sums[:, LANES * i : LANES * (i + 1)] for i in range(2 * runs[c])]
        gate = lax.concatenate(columns[::2], 1)
        up = lax.concatenate(columns[1::2], 1)
        return (jax.nn.silu(gate) * up).astype(jnp.bfloat16)

    def addend(slot, far, parts, wide):
        c = slot - far
        if c < chunks:
            return fit(parts[max(c, 0)], wide)
        k = c - first
        if far == 0 and 0 <= k < sends:
            return fit(packed[k], wide)
        return jnp.zeros((rows, wide), jnp.bfloat16)

    def dots(whole, c):
        return tuple(first_dots(whole, gate_weight, up_weight, starts[c], runs[c]))

    delays = {0: 0, chunks - 3: 1, chunks - 2: 1}

    def ahead(whole, slot):
        c = slot + 1
        return lax.cond(
            core == delays[slot],
            lambda w: dots(w, c),
            lambda w: (jnp.zeros((rows, 2 * size([c])), jnp.bfloat16),) * 2,
            whole,
        )

    def after(whole, slot, early):
        return lax.cond(core == delays[slot], lambda w, e: e, lambda w, e: dots(w, slot + 1), whole, early)

    whole = gather_features(inputs, index, count)
    low[0], high[0] = dots(whole, 0)
    for slot in range(slots):
        wide = width(slot)
        up = choose(z, [addend(slot, min(v, n - 2), high, wide) for v in range(n)])
        down = choose(back, [addend(slot, min(v, n - 2), low, wide) for v in range(n)])
        if slot > 0:
            up = up + fit(from_below[slot - 1], wide)
            down = down + fit(from_above[slot - 1], wide)
        early = None
        if slot in delays:
            whole, up, down = lax.optimization_barrier((whole, up, down))
            early = ahead(whole, slot)
        whole, up, down, early = lax.optimization_barrier((whole, up, down, early))
        from_below[slot] = lax.ppermute(up, "gx", up_pairs)
        from_above[slot] = lax.ppermute(down, "gx", down_pairs)
        if slot in delays:
            low[slot + 1], high[slot + 1] = after(whole, slot, early)
        elif slot + 1 < chunks:
            low[slot + 1], high[slot + 1] = dots(whole, slot + 1)

        from_below[slot], from_above[slot], low[slot + 1], terms[slot - 1] = lax.optimization_barrier(
            (from_below[slot], from_above[slot], low.get(slot + 1), terms.get(slot - 1))
        )

        c = slot - (n - 2)
        if 0 <= c < chunks:
            hidden[c] = make_hidden(c)
            for k, members in enumerate(pieces):
                if members[-1] == c:
                    packed[k] = lax.concatenate([hidden[m] for m in members], 1)

        k = slot - (first + n - 2)
        if 0 <= k < sends:
            wide = packed[k].shape[1]
            lower = choose(z, [packed[k]] + [fit(from_below[first + k + v], wide) for v in range(n - 1)])
            upper = choose(back, [packed[k]] + [fit(from_above[first + k + v], wide) for v in range(n - 1)])
            at = 2 * LANES * starts[pieces[k][0]]
            if k < sends - 1:
                terms[slot] = down_dots(lower, upper, down_weight, terms.get(slot - 1), at)

    total = terms.get(slots - 2)
    if total is None:
        total = jnp.zeros((rows, down_weight.shape[1]), jnp.float32)
    for half in range(2):
        top, bottom = rows // 2 * half, rows // 2 * (half + 1)
        left, right = lower[top:bottom], upper[top:bottom]
        if down_weight.shape[1] // count % LANES == 0:
            give, keep = last_dots(left, right, down_weight, total, place, at, half)
        else:
            give, keep = split_columns(
                down_dots(left, right, down_weight, total[top:bottom], at), core, count
            )
        results.append(add_chips(scatter_chips(chip_sums(give, keep, count), index // 2, count), count))
    return lax.concatenate(results, 0)


def solution(mesh):
    return jax.shard_map(
        functools.partial(shards, n=mesh.shape["gx"], count=mesh.shape["yz"]),
        mesh=mesh,
        in_specs=(P("rep", ("gx", "yz")), P("gx", "yz"), P("gx", "yz"), P("yz", "gx")),
        out_specs=P("rep", ("gx", "yz")),
        check_vma=False,
    )
```

```python
import functools

import jax
import jax.numpy as jnp
from jax import lax
from jax.experimental import pallas as pl
from jax.experimental.pallas import tpu as pltpu
from jax.sharding import PartitionSpec as P

LANES = 128
UNITS = 4


def choose(index, cases):
    if all(case is cases[0] for case in cases):
        return cases[0]
    return lax.select_n(index, *cases)


def gather_features(own, index, count):
    pair = [(i, i ^ 1) for i in range(count)]
    chips = count // 2
    core, chip = index % 2, index // 2
    far = [own]
    for _ in range(chips - 1):
        far.append(lax.ppermute(far[-1], "yz", [(i, (i + 2) % count) for i in range(count)]))
    near = [lax.ppermute(block, "yz", pair) for block in far]
    blocks = []
    for j in range(chips):
        mine = choose(chip, [far[(v - j) % chips] for v in range(chips)])
        other = choose(chip, [near[(v - j) % chips] for v in range(chips)])
        blocks += [choose(core, [mine, other]), choose(core, [other, mine])]
    return lax.concatenate(blocks, 1)


def spread_units(lower_ref, upper_ref, held_ref):
    for i in range(lower_ref.shape[1] // LANES):
        held_ref[:, 2 * LANES * i : 2 * LANES * i + LANES] = lower_ref[:, LANES * i : LANES * (i + 1)]
        held_ref[:, 2 * LANES * i + LANES : 2 * LANES * (i + 1)] = upper_ref[:, LANES * i : LANES * (i + 1)]


def down_dots(lower, upper, down_weight, base, start):
    rows, size = lower.shape
    total = down_weight.shape[1]
    depth, wide = 2 * size, min(total, 4 * LANES)

    def kernel(lower_ref, upper_ref, weight_ref, *refs):
        out_ref, held_ref = refs[-2:]

        @pl.when(pl.program_id(0) == 0)
        def _():
            spread_units(lower_ref, upper_ref, held_ref)

        term = jnp.dot(held_ref[...], weight_ref[...], preferred_element_type=jnp.float32)
        out_ref[...] = term + refs[0][...] if len(refs) > 2 else term

    here = pl.BlockSpec((rows, size), lambda step: (0, 0))
    block = pl.BlockSpec((rows, wide), lambda step: (0, step))
    weight = pl.BlockSpec((pl.Element(depth), pl.Element(wide)), lambda step: (start, step * wide))
    given = [] if base is None else [base]
    return pl.pallas_call(
        kernel,
        grid=(total // wide,),
        in_specs=[here, here, weight] + [block] * len(given),
        out_specs=block,
        out_shape=jax.ShapeDtypeStruct((rows, total), jnp.float32),
        scratch_shapes=[pltpu.VMEM((rows, depth), jnp.bfloat16)],
        compiler_params=pltpu.CompilerParams(vmem_limit_bytes=40 * 1024 * 1024),
        cost_estimate=pl.CostEstimate(flops=0, bytes_accessed=0, transcendentals=0),
    )(lower, upper, down_weight, *given)


def last_dots(lower, upper, down_weight, base, place, start, block):
    rows, size = lower.shape
    total = down_weight.shape[1]
    depth, wide = 2 * size, total // place.shape[0]
    steps = place.shape[0]

    def kernel(place_ref, lower_ref, upper_ref, weight_ref, base_ref, give_ref, keep_ref, held_ref):
        spread_units(lower_ref, upper_ref, held_ref)
        for step in range(steps):
            columns = pl.ds(pl.multiple_of(place_ref[step] * wide, wide), wide)
            term = jnp.dot(held_ref[...], weight_ref[:, columns], preferred_element_type=jnp.float32)
            result = (term + base_ref[:, columns]).astype(jnp.bfloat16)
            out_ref, at = (give_ref, step) if step < steps // 2 else (keep_ref, step - steps // 2)
            out_ref[:, wide * at : wide * (at + 1)] = result

    here = pl.BlockSpec((rows, size), lambda i, place: (0, 0))
    out = pl.BlockSpec((rows, total // 2), lambda i, place: (0, 0))
    return pl.pallas_call(
        kernel,
        grid_spec=pltpu.PrefetchScalarGridSpec(
            num_scalar_prefetch=1,
            grid=(1,),
            in_specs=[
                here,
                here,
                pl.BlockSpec((pl.Element(depth), pl.Element(total)), lambda i, place: (start, 0)),
                pl.BlockSpec((rows, total), lambda i, place: (block, 0)),
            ],
            out_specs=[out, out],
            scratch_shapes=[pltpu.VMEM((rows, depth), jnp.bfloat16)],
        ),
        out_shape=[jax.ShapeDtypeStruct((rows, total // 2), jnp.bfloat16)] * 2,
        compiler_params=pltpu.CompilerParams(vmem_limit_bytes=40 * 1024 * 1024),
        cost_estimate=pl.CostEstimate(
            flops=2 * rows * depth * total, bytes_accessed=2 * depth * total + 6 * rows * total, transcendentals=0
        ),
    )(place, lower, upper, down_weight, base)


def split_columns(total, core, count):
    share = total.shape[1] // count
    blocks = [total[:, share * i : share * (i + 1)].astype(jnp.bfloat16) for i in range(count)]
    return [
        lax.concatenate([choose(c, [blocks[2 * j], blocks[2 * j + 1]]) for j in range(count // 2)], 1)
        for c in (1 - core, core)
    ]


def chip_sums(give, keep, count):
    got = lax.ppermute(give, "yz", [(i, i ^ 1) for i in range(count)])
    return (keep.astype(jnp.float32) + got.astype(jnp.float32)).astype(jnp.bfloat16)


def scatter_chips(sums, chip, count):
    chips = count // 2
    share = sums.shape[1] // chips
    blocks = [sums[:, share * j : share * (j + 1)] for j in range(chips)]
    return [choose(chip, [blocks[(v + k) % chips] for v in range(chips)]) for k in range(chips)]


def add_chips(sends, count):
    result = sends[0].astype(jnp.float32)
    for k, send in enumerate(sends[1:], 1):
        moved = lax.ppermute(send, "yz", [(i, (i + 2 * k) % count) for i in range(count)])
        result = result + moved.astype(jnp.float32)
    return result.astype(jnp.bfloat16)


def first_dots(features, gate_weight, up_weight, start, units):
    rows, depth = features.shape

    def kernel(x_ref, gate_ref, up_ref, low_ref, high_ref):
        gate = jnp.dot(x_ref[...], gate_ref[...], preferred_element_type=jnp.float32).astype(jnp.bfloat16)
        low_ref[:, :LANES] = gate[:, :LANES]
        high_ref[:, :LANES] = gate[:, LANES:]
        up = jnp.dot(x_ref[...], up_ref[...], preferred_element_type=jnp.float32).astype(jnp.bfloat16)
        low_ref[:, LANES:] = up[:, :LANES]
        high_ref[:, LANES:] = up[:, LANES:]

    weight = pl.BlockSpec((depth, 2 * LANES), lambda j: (0, start + j))
    out = pl.BlockSpec((rows, 2 * LANES), lambda j: (0, j))
    wide = 2 * LANES * units
    return pl.pallas_call(
        kernel,
        grid=(units,),
        in_specs=[pl.BlockSpec((rows, depth), lambda j: (0, 0)), weight, weight],
        out_specs=[out, out],
        out_shape=[jax.ShapeDtypeStruct((rows, wide), jnp.bfloat16)] * 2,
        compiler_params=pltpu.CompilerParams(vmem_limit_bytes=32 * 1024 * 1024),
        cost_estimate=pl.CostEstimate(
            flops=0,
            bytes_accessed=0,
            transcendentals=0,
        ),
    )(features, gate_weight, up_weight)


def shards(inputs, gate_weight, up_weight, down_weight, *, n, count):
    index = lax.axis_index("yz")
    core = index % 2
    z = lax.axis_index("gx")
    back = n - 1 - z
    inner = (z > 0).astype(jnp.int32)
    rows = inputs.shape[0]
    units = gate_weight.shape[1] // (2 * LANES)
    runs = ([units % UNITS] if units % UNITS else []) + [UNITS] * (units // UNITS)
    chunks = len(runs)
    starts = [sum(runs[:c]) for c in range(chunks)]
    pieces = [list(range(c, min(c + 2, chunks))) for c in range(0, chunks, 2)]
    sends = len(pieces)
    first = max([chunks] + [piece[-1] + n - 1 - k for k, piece in enumerate(pieces)])
    slots = first + sends + n - 2
    up_pairs = [(i, i + 1) for i in range(n - 1)]
    down_pairs = [(i + 1, i) for i in range(n - 1)]

    def size(members):
        return LANES * sum(runs[m] for m in members)

    def width(slot):
        active = [slot - v for v in range(n - 1)]
        wide = [2 * size([c]) for c in active if 0 <= c < chunks]
        wide += [size(pieces[c - first]) for c in active if 0 <= c - first < sends]
        return max(wide)

    def fit(array, wide):
        if array.shape[1] < wide:
            return jnp.pad(array, ((0, 0), (0, wide - array.shape[1])))
        return array[:, :wide]

    low, high = {}, {}
    from_below, from_above, packed, terms, hidden = {}, {}, {}, {}, {}
    results = []
    place = jnp.stack([2 * j + c for c in (1 - core, core) for j in range(count // 2)]).astype(jnp.int32)

    def make_hidden(c):
        got = choose(inner, [from_above[c + n - 2], from_below[c + n - 2]])
        own = choose(inner, [low[c], high[c]])
        sums = got[:, : 2 * size([c])].astype(jnp.float32) + own.astype(jnp.float32)
        columns = [sums[:, LANES * i : LANES * (i + 1)] for i in range(2 * runs[c])]
        gate = lax.concatenate(columns[::2], 1)
        up = lax.concatenate(columns[1::2], 1)
        return (jax.nn.silu(gate) * up).astype(jnp.bfloat16)

    def addend(slot, far, parts, wide):
        c = slot - far
        if c < chunks:
            return fit(parts[max(c, 0)], wide)
        k = c - first
        if far == 0 and 0 <= k < sends:
            return fit(packed[k], wide)
        return jnp.zeros((rows, wide), jnp.bfloat16)

    def dots(whole, c):
        return tuple(first_dots(whole, gate_weight, up_weight, starts[c], runs[c]))

    delays = {0: 0}

    def ahead(whole, slot):
        c = slot + 1
        return lax.cond(
            core == delays[slot],
            lambda w: dots(w, c),
            lambda w: (jnp.zeros((rows, 2 * size([c])), jnp.bfloat16),) * 2,
            whole,
        )

    def after(whole, slot, early):
        return lax.cond(core == delays[slot], lambda w, e: e, lambda w, e: dots(w, slot + 1), whole, early)

    whole = gather_features(inputs, index, count)
    low[0], high[0] = dots(whole, 0)
    for slot in range(slots):
        wide = width(slot)
        up = choose(z, [addend(slot, min(v, n - 2), high, wide) for v in range(n)])
        down = choose(back, [addend(slot, min(v, n - 2), low, wide) for v in range(n)])
        if slot > 0:
            up = up + fit(from_below[slot - 1], wide)
            down = down + fit(from_above[slot - 1], wide)
        early = None
        if slot in delays:
            whole, up, down = lax.optimization_barrier((whole, up, down))
            early = ahead(whole, slot)
        whole, up, down, early = lax.optimization_barrier((whole, up, down, early))
        from_below[slot] = lax.ppermute(up, "gx", up_pairs)
        from_above[slot] = lax.ppermute(down, "gx", down_pairs)
        if slot in delays:
            low[slot + 1], high[slot + 1] = after(whole, slot, early)
        elif slot + 1 < chunks:
            low[slot + 1], high[slot + 1] = dots(whole, slot + 1)

        from_below[slot], from_above[slot], low[slot + 1], terms[slot - 1] = lax.optimization_barrier(
            (from_below[slot], from_above[slot], low.get(slot + 1), terms.get(slot - 1))
        )

        c = slot - (n - 2)
        if 0 <= c < chunks:
            hidden[c] = make_hidden(c)
            for k, members in enumerate(pieces):
                if members[-1] == c:
                    packed[k] = lax.concatenate([hidden[m] for m in members], 1)

        k = slot - (first + n - 2)
        if 0 <= k < sends:
            wide = packed[k].shape[1]
            lower = choose(z, [packed[k]] + [fit(from_below[first + k + v], wide) for v in range(n - 1)])
            upper = choose(back, [packed[k]] + [fit(from_above[first + k + v], wide) for v in range(n - 1)])
            at = 2 * LANES * starts[pieces[k][0]]
            if k < sends - 1:
                terms[slot] = down_dots(lower, upper, down_weight, terms.get(slot - 1), at)

    total = terms.get(slots - 2)
    if total is None:
        total = jnp.zeros((rows, down_weight.shape[1]), jnp.float32)
    for half in range(2):
        top, bottom = rows // 2 * half, rows // 2 * (half + 1)
        left, right = lower[top:bottom], upper[top:bottom]
        if down_weight.shape[1] // count % LANES == 0:
            give, keep = last_dots(left, right, down_weight, total, place, at, half)
        else:
            give, keep = split_columns(
                down_dots(left, right, down_weight, total[top:bottom], at), core, count
            )
        results.append(add_chips(scatter_chips(chip_sums(give, keep, count), index // 2, count), count))
    return lax.concatenate(results, 0)


def solution(mesh):
    return jax.shard_map(
        functools.partial(shards, n=mesh.shape["gx"], count=mesh.shape["yz"]),
        mesh=mesh,
        in_specs=(P("rep", ("gx", "yz")), P("gx", "yz"), P("gx", "yz"), P("yz", "gx")),
        out_specs=P("rep", ("gx", "yz")),
        check_vma=False,
    )
```

```python
import functools

import jax
import jax.numpy as jnp
from jax import lax
from jax.experimental import pallas as pl
from jax.experimental.pallas import tpu as pltpu
from jax.sharding import PartitionSpec as P

LANES = 128
UNITS = 4


def choose(index, cases):
    if all(case is cases[0] for case in cases):
        return cases[0]
    return lax.select_n(index, *cases)


def gather_features(own, index, count):
    pair = [(i, i ^ 1) for i in range(count)]
    chips = count // 2
    core, chip = index % 2, index // 2
    far = [own]
    for _ in range(chips - 1):
        far.append(lax.ppermute(far[-1], "yz", [(i, (i + 2) % count) for i in range(count)]))
    near = [lax.ppermute(block, "yz", pair) for block in far]
    blocks = []
    for j in range(chips):
        mine = choose(chip, [far[(v - j) % chips] for v in range(chips)])
        other = choose(chip, [near[(v - j) % chips] for v in range(chips)])
        blocks += [choose(core, [mine, other]), choose(core, [other, mine])]
    return lax.concatenate(blocks, 1)


def spread_units(lower_ref, upper_ref, held_ref):
    for i in range(lower_ref.shape[1] // LANES):
        held_ref[:, 2 * LANES * i : 2 * LANES * i + LANES] = lower_ref[:, LANES * i : LANES * (i + 1)]
        held_ref[:, 2 * LANES * i + LANES : 2 * LANES * (i + 1)] = upper_ref[:, LANES * i : LANES * (i + 1)]


def down_dots(lower, upper, down_weight, base, start):
    rows, size = lower.shape
    total = down_weight.shape[1]
    depth, wide = 2 * size, min(total, 4 * LANES)

    def kernel(lower_ref, upper_ref, weight_ref, *refs):
        out_ref, held_ref = refs[-2:]

        @pl.when(pl.program_id(0) == 0)
        def _():
            spread_units(lower_ref, upper_ref, held_ref)

        term = jnp.dot(held_ref[...], weight_ref[...], preferred_element_type=jnp.float32)
        out_ref[...] = term + refs[0][...] if len(refs) > 2 else term

    here = pl.BlockSpec((rows, size), lambda step: (0, 0))
    block = pl.BlockSpec((rows, wide), lambda step: (0, step))
    weight = pl.BlockSpec((pl.Element(depth), pl.Element(wide)), lambda step: (start, step * wide))
    given = [] if base is None else [base]
    return pl.pallas_call(
        kernel,
        grid=(total // wide,),
        in_specs=[here, here, weight] + [block] * len(given),
        out_specs=block,
        out_shape=jax.ShapeDtypeStruct((rows, total), jnp.float32),
        scratch_shapes=[pltpu.VMEM((rows, depth), jnp.bfloat16)],
        compiler_params=pltpu.CompilerParams(vmem_limit_bytes=40 * 1024 * 1024),
        cost_estimate=pl.CostEstimate(flops=0, bytes_accessed=0, transcendentals=0),
    )(lower, upper, down_weight, *given)


def last_dots(lower, upper, down_weight, base, place, start, block):
    rows, size = lower.shape
    total = down_weight.shape[1]
    depth, wide = 2 * size, total // place.shape[0]
    steps = place.shape[0]

    def kernel(place_ref, lower_ref, upper_ref, weight_ref, base_ref, give_ref, keep_ref, held_ref):
        spread_units(lower_ref, upper_ref, held_ref)
        for step in range(steps):
            columns = pl.ds(pl.multiple_of(place_ref[step] * wide, wide), wide)
            term = jnp.dot(held_ref[...], weight_ref[:, columns], preferred_element_type=jnp.float32)
            result = (term + base_ref[:, columns]).astype(jnp.bfloat16)
            out_ref, at = (give_ref, step) if step < steps // 2 else (keep_ref, step - steps // 2)
            out_ref[:, wide * at : wide * (at + 1)] = result

    here = pl.BlockSpec((rows, size), lambda i, place: (0, 0))
    out = pl.BlockSpec((rows, total // 2), lambda i, place: (0, 0))
    return pl.pallas_call(
        kernel,
        grid_spec=pltpu.PrefetchScalarGridSpec(
            num_scalar_prefetch=1,
            grid=(1,),
            in_specs=[
                here,
                here,
                pl.BlockSpec((pl.Element(depth), pl.Element(total)), lambda i, place: (start, 0)),
                pl.BlockSpec((rows, total), lambda i, place: (block, 0)),
            ],
            out_specs=[out, out],
            scratch_shapes=[pltpu.VMEM((rows, depth), jnp.bfloat16)],
        ),
        out_shape=[jax.ShapeDtypeStruct((rows, total // 2), jnp.bfloat16)] * 2,
        compiler_params=pltpu.CompilerParams(vmem_limit_bytes=40 * 1024 * 1024),
        cost_estimate=pl.CostEstimate(
            flops=2 * rows * depth * total, bytes_accessed=2 * depth * total + 6 * rows * total, transcendentals=0
        ),
    )(place, lower, upper, down_weight, base)


def split_columns(total, core, count):
    share = total.shape[1] // count
    blocks = [total[:, share * i : share * (i + 1)].astype(jnp.bfloat16) for i in range(count)]
    return [
        lax.concatenate([choose(c, [blocks[2 * j], blocks[2 * j + 1]]) for j in range(count // 2)], 1)
        for c in (1 - core, core)
    ]


def chip_sums(give, keep, count):
    got = lax.ppermute(give, "yz", [(i, i ^ 1) for i in range(count)])
    return (keep.astype(jnp.float32) + got.astype(jnp.float32)).astype(jnp.bfloat16)


def scatter_chips(sums, chip, count):
    chips = count // 2
    share = sums.shape[1] // chips
    blocks = [sums[:, share * j : share * (j + 1)] for j in range(chips)]
    return [choose(chip, [blocks[(v + k) % chips] for v in range(chips)]) for k in range(chips)]


def add_chips(sends, count):
    result = sends[0].astype(jnp.float32)
    for k, send in enumerate(sends[1:], 1):
        moved = lax.ppermute(send, "yz", [(i, (i + 2 * k) % count) for i in range(count)])
        result = result + moved.astype(jnp.float32)
    return result.astype(jnp.bfloat16)


def first_dots(features, gate_weight, up_weight, start, units):
    rows, depth = features.shape

    def kernel(x_ref, gate_ref, up_ref, low_ref, high_ref):
        gate = jnp.dot(x_ref[...], gate_ref[...], preferred_element_type=jnp.float32).astype(jnp.bfloat16)
        low_ref[:, :LANES] = gate[:, :LANES]
        high_ref[:, :LANES] = gate[:, LANES:]
        up = jnp.dot(x_ref[...], up_ref[...], preferred_element_type=jnp.float32).astype(jnp.bfloat16)
        low_ref[:, LANES:] = up[:, :LANES]
        high_ref[:, LANES:] = up[:, LANES:]

    weight = pl.BlockSpec((depth, 2 * LANES), lambda j: (0, start + j))
    out = pl.BlockSpec((rows, 2 * LANES), lambda j: (0, j))
    wide = 2 * LANES * units
    return pl.pallas_call(
        kernel,
        grid=(units,),
        in_specs=[pl.BlockSpec((rows, depth), lambda j: (0, 0)), weight, weight],
        out_specs=[out, out],
        out_shape=[jax.ShapeDtypeStruct((rows, wide), jnp.bfloat16)] * 2,
        compiler_params=pltpu.CompilerParams(vmem_limit_bytes=32 * 1024 * 1024),
        cost_estimate=pl.CostEstimate(
            flops=0,
            bytes_accessed=0,
            transcendentals=0,
        ),
    )(features, gate_weight, up_weight)


def shards(inputs, gate_weight, up_weight, down_weight, *, n, count):
    index = lax.axis_index("yz")
    core = index % 2
    z = lax.axis_index("gx")
    back = n - 1 - z
    inner = (z > 0).astype(jnp.int32)
    rows = inputs.shape[0]
    units = gate_weight.shape[1] // (2 * LANES)
    runs = ([units % UNITS] if units % UNITS else []) + [UNITS] * (units // UNITS)
    chunks = len(runs)
    starts = [sum(runs[:c]) for c in range(chunks)]
    pieces = [list(range(c, min(c + 2, chunks))) for c in range(0, chunks, 2)]
    sends = len(pieces)
    first = max([chunks] + [piece[-1] + n - 1 - k for k, piece in enumerate(pieces)])
    slots = first + sends + n - 2
    up_pairs = [(i, i + 1) for i in range(n - 1)]
    down_pairs = [(i + 1, i) for i in range(n - 1)]

    def size(members):
        return LANES * sum(runs[m] for m in members)

    def width(slot):
        active = [slot - v for v in range(n - 1)]
        wide = [2 * size([c]) for c in active if 0 <= c < chunks]
        wide += [size(pieces[c - first]) for c in active if 0 <= c - first < sends]
        return max(wide)

    def fit(array, wide):
        if array.shape[1] < wide:
            return jnp.pad(array, ((0, 0), (0, wide - array.shape[1])))
        return array[:, :wide]

    low, high = {}, {}
    from_below, from_above, packed, terms, hidden = {}, {}, {}, {}, {}
    results = []
    place = jnp.stack([2 * j + c for c in (1 - core, core) for j in range(count // 2)]).astype(jnp.int32)

    def make_hidden(c):
        got = choose(inner, [from_above[c + n - 2], from_below[c + n - 2]])
        own = choose(inner, [low[c], high[c]])
        sums = got[:, : 2 * size([c])].astype(jnp.float32) + own.astype(jnp.float32)
        columns = [sums[:, LANES * i : LANES * (i + 1)] for i in range(2 * runs[c])]
        gate = lax.concatenate(columns[::2], 1)
        up = lax.concatenate(columns[1::2], 1)
        return (jax.nn.silu(gate) * up).astype(jnp.bfloat16)

    def addend(slot, far, parts, wide):
        c = slot - far
        if c < chunks:
            return fit(parts[max(c, 0)], wide)
        k = c - first
        if far == 0 and 0 <= k < sends:
            return fit(packed[k], wide)
        return jnp.zeros((rows, wide), jnp.bfloat16)

    def dots(whole, c):
        return tuple(first_dots(whole, gate_weight, up_weight, starts[c], runs[c]))

    delays = {0: (0, runs[1]), chunks - 2: (1, 1)}

    def some(whole, c, begin, end):
        return tuple(first_dots(whole, gate_weight, up_weight, starts[c] + begin, end - begin))

    def ahead(whole, slot):
        late, part = delays[slot]
        return lax.cond(
            core == late,
            lambda w: some(w, slot + 1, 0, part),
            lambda w: (jnp.zeros((rows, 2 * LANES * part), jnp.bfloat16),) * 2,
            whole,
        )

    def after(whole, slot, early):
        late, part = delays[slot]
        c = slot + 1
        done = lax.cond(core == late, lambda w, e: e, lambda w, e: some(w, c, 0, part), whole, early)
        if part == runs[c]:
            return done
        return [lax.concatenate(both, 1) for both in zip(done, some(whole, c, part, runs[c]))]

    whole = gather_features(inputs, index, count)
    low[0], high[0] = dots(whole, 0)
    for slot in range(slots):
        wide = width(slot)
        up = choose(z, [addend(slot, min(v, n - 2), high, wide) for v in range(n)])
        down = choose(back, [addend(slot, min(v, n - 2), low, wide) for v in range(n)])
        if slot > 0:
            up = up + fit(from_below[slot - 1], wide)
            down = down + fit(from_above[slot - 1], wide)
        early = None
        if slot in delays:
            whole, up, down = lax.optimization_barrier((whole, up, down))
            early = ahead(whole, slot)
        whole, up, down, early = lax.optimization_barrier((whole, up, down, early))
        from_below[slot] = lax.ppermute(up, "gx", up_pairs)
        from_above[slot] = lax.ppermute(down, "gx", down_pairs)
        if slot in delays:
            low[slot + 1], high[slot + 1] = after(whole, slot, early)
        elif slot + 1 < chunks:
            low[slot + 1], high[slot + 1] = dots(whole, slot + 1)

        from_below[slot], from_above[slot], low[slot + 1], terms[slot - 1] = lax.optimization_barrier(
            (from_below[slot], from_above[slot], low.get(slot + 1), terms.get(slot - 1))
        )

        c = slot - (n - 2)
        if 0 <= c < chunks:
            hidden[c] = make_hidden(c)
            for k, members in enumerate(pieces):
                if members[-1] == c:
                    packed[k] = lax.concatenate([hidden[m] for m in members], 1)

        k = slot - (first + n - 2)
        if 0 <= k < sends:
            wide = packed[k].shape[1]
            lower = choose(z, [packed[k]] + [fit(from_below[first + k + v], wide) for v in range(n - 1)])
            upper = choose(back, [packed[k]] + [fit(from_above[first + k + v], wide) for v in range(n - 1)])
            at = 2 * LANES * starts[pieces[k][0]]
            if k < sends - 1:
                terms[slot] = down_dots(lower, upper, down_weight, terms.get(slot - 1), at)

    total = terms.get(slots - 2)
    if total is None:
        total = jnp.zeros((rows, down_weight.shape[1]), jnp.float32)
    for half in range(2):
        top, bottom = rows // 2 * half, rows // 2 * (half + 1)
        left, right = lower[top:bottom], upper[top:bottom]
        if down_weight.shape[1] // count % LANES == 0:
            give, keep = last_dots(left, right, down_weight, total, place, at, half)
        else:
            give, keep = split_columns(
                down_dots(left, right, down_weight, total[top:bottom], at), core, count
            )
        results.append(add_chips(scatter_chips(chip_sums(give, keep, count), index // 2, count), count))
    return lax.concatenate(results, 0)


def solution(mesh):
    return jax.shard_map(
        functools.partial(shards, n=mesh.shape["gx"], count=mesh.shape["yz"]),
        mesh=mesh,
        in_specs=(P("rep", ("gx", "yz")), P("gx", "yz"), P("gx", "yz"), P("yz", "gx")),
        out_specs=P("rep", ("gx", "yz")),
        check_vma=False,
    )
```
